512 devices in a mesh: row: 32 (over y_lo, z), col: 16 (over x, y_hi, core).
Axes of the slice: x: 4, y: 4 (y_hi: 2, y_lo: 2; y = y_hi * 2 + y_lo), z: 16, core: 2. Of those that a mesh axis runs over, the one named last changes fastest.
Arguments:
- bra_density: bfloat16 [8192, 12288], P('row', 'col'), may hold values from -6 to 6
- ket_density: bfloat16 [8192, 12288], P('col', 'row'), may hold values from -6 to 6
- coulomb: float32 [12288], replicated, may hold values from 0.002 to 0.02
- cond_pairs: bfloat16 [256, 8, 32, 256], P('row'), may hold values from -1 to 1
- val_pairs: bfloat16 [8, 32, 256, 256], P(None, None, 'col'), may hold values from -6 to 6
- screened: bfloat16 [16, 256, 256], P('col'), may hold values from -0.375 to 0.375
- q_owner: int32 [8, 8], replicated, may hold values from 0 to 15
- g_shift: int32 [8, 8, 256], replicated, may hold values from 0 to 255, each once within a row
Outputs:
- kernel: float32 [8192, 8192], P('row', 'col')
The draws below stay inside these ranges and needn't reach their ends.
Inputs may be any that keep to these rules, and one draw needn't show every extreme that they name: `g_shift`: each row of the last dimension is a permutation of 0 to 255.
All inputs are finite; a program needn't handle non-finite values.
Results may differ from the reference program's by a relative error of at most 0.0029.
Values may be sent and summed in bfloat16 or wider, within the bound.
No kernel may reach another device: no remote copies, remote signals or barrier semaphores. Data moves between devices by JAX's collectives and lax.ppermute only.
A program may use at most 64 MiB of HBM per device.

```python
import math
import jax
import jax.numpy as jnp
from jax import lax

NV = 32
NC = 32
NG = 12288
NGW = 256
CB = 8
VB = 16
NKB = 8
NKK = 8
NQ = 16
ROWS_B = 8192
ROWS_K = 8192
N_ROW = 32
N_COL = 16


def plant(array, rng, smallest, largest):
    longest = array.shape.index(max(array.shape))
    spots = []
    for shift in (0, 1):
        where = [jax.random.randint(jax.random.fold_in(rng, axis), (), 0, length) for axis, length in enumerate(array.shape)]
        where[longest] = (where[longest] + shift) % array.shape[longest]
        spots.append(tuple(where))
    return array.at[spots[0]].set(smallest).at[spots[1]].set(largest)


def level_of(stream_key, shape, cuts, smallest, top_value):
    def one(position, shards_of):
        steps = jax.random.uniform(jax.random.fold_in(jax.random.fold_in(stream_key, 6), position), (shards_of,), jnp.float32, smallest / len(cuts), top_value / len(cuts))
        return jnp.repeat(jnp.exp(steps), shape[position] // shards_of).reshape((-1,) + (1,) * (len(shape) - position - 1))

    loudness = one(*cuts[0])
    for cut in cuts[1:]:
        loudness = loudness * one(*cut)
    return loudness


def bell_draw(key, extent, scale, limit, shards=(), kind=jnp.bfloat16):
    values = jax.random.normal(key, extent, jnp.float32) * scale
    if len(shards) > 0:
        values = level_of(key, extent, shards, -0.22, 0.18) * values
    return jnp.clip(values, min=-limit, max=limit).astype(kind)


def setup_inputs(seed: int = 0) -> dict:
    arg_keys = jax.random.split(jax.random.key(seed), 9)
    bra_density = bell_draw(arg_keys[0], (ROWS_B, NG), 1.0, 6.0, ((0, 32), (1, 16)))
    ket_density = bell_draw(arg_keys[1], (ROWS_K, NG), 1.0, 6.0, ((0, 16), (1, 32)))
    coulomb = jnp.clip(jnp.exp(jax.random.uniform(arg_keys[2], (NG,), jnp.float32, math.log(0.002), math.log(0.02))), 0.002, 0.02)
    cond_pairs = bell_draw(arg_keys[3], (N_ROW * CB, NKK, NC, NGW), 0.0625, 1.0, ((0, 32),))
    val_pairs = bell_draw(arg_keys[4], (NKB, NV, N_COL * VB, NGW), 1.0, 6.0, ((2, 16),))
    screened = bell_draw(arg_keys[5], (NQ, NGW, NGW), NGW ** -0.5, 0.375, ((0, 16),))
    q_owner = plant(jax.random.randint(arg_keys[6], (NKB, NKK), 0, N_COL), jax.random.fold_in(arg_keys[6], 1), 0, N_COL - 1).astype(jnp.int32)
    g_shift = jax.vmap(lambda own: jax.random.permutation(own, NGW))(jax.random.split(arg_keys[7], NKB * NKK)).reshape((NKB, NKK, NGW)).astype(jnp.int32)
    return dict(bra_density=bra_density, ket_density=ket_density, coulomb=coulomb, cond_pairs=cond_pairs, val_pairs=val_pairs, screened=screened, q_owner=q_owner, g_shift=g_shift)


def reference(bra_density, ket_density, coulomb, cond_pairs, val_pairs, screened, q_owner, g_shift):
    scaled = (bra_density.astype(jnp.float32) * coulomb[None, :]).astype(jnp.bfloat16)
    exchange = jnp.dot(scaled, ket_density.T, preferred_element_type=jnp.float32)
    n_row = bra_density.shape[0] // (NV * CB)
    n_col = ket_density.shape[0] // (VB * NC)
    per_bra = NC // CB
    per_ket = NV // VB

    def block(flat):
        brow = flat // n_col
        bcol = flat % n_col
        kbra = brow // per_bra
        kket = bcol // per_ket
        q_index = q_owner[kbra, kket]
        perm = g_shift[kbra, kket]
        vals = lax.dynamic_index_in_dim(val_pairs, kbra, 0, keepdims=False)
        vals = lax.dynamic_slice_in_dim(vals, (bcol * VB).astype(jnp.int32), VB, 1)
        shifted = jnp.take(vals, perm, axis=2).reshape(NV * VB, NGW)
        w_block = lax.dynamic_index_in_dim(screened, q_index, 0, keepdims=False)
        pairs = lax.dot_general(shifted, w_block, (((1,), (1,)), ((), ())), preferred_element_type=jnp.float32)
        pairs = pairs.astype(jnp.bfloat16).reshape(NV, VB, NGW)
        conds = lax.dynamic_slice_in_dim(cond_pairs, (brow * CB).astype(jnp.int32), CB, 0)
        conds = lax.dynamic_index_in_dim(conds, kket, 1, keepdims=False)
        direct = jnp.einsum('xcg,vug->vxuc', conds.astype(jnp.float32), pairs.astype(jnp.float32))
        return direct.reshape(NV * CB, VB * NC)

    blocks = lax.map(block, jnp.arange(n_row * n_col, dtype=jnp.int32))
    blocks = blocks.reshape(n_row, n_col, NV * CB, VB * NC).transpose(0, 2, 1, 3)
    direct = blocks.reshape(n_row * NV * CB, n_col * VB * NC)
    return 2.0 * exchange - direct
```

```python
import jax
import jax.numpy as jnp
from jax import lax
from jax.experimental import pallas as pl
from jax.experimental.pallas import tpu as pltpu
from jax.sharding import Mesh, PartitionSpec as P

AXES = ("ylo", "z", "x", "yhi", "core")
SIZES = (2, 16, 4, 2, 2)
ROW = ("ylo", "z")
COL = ("x", "yhi", "core")


def flat(place):
    index = 0
    for at, size in zip(place, SIZES):
        index = index * size + at
    return index


def permute(array, target):
    pairs = []
    for ylo in range(2):
        for z in range(16):
            for x in range(4):
                for yhi in range(2):
                    for core in range(2):
                        place = (ylo, z, x, yhi, core)
                        pairs.append((flat(place), flat(target(*place))))
    return lax.ppermute(array, AXES, pairs)


def product_t(a, b):
    return lax.dot_general(a, b, (((1,), (1,)), ((), ())), preferred_element_type=jnp.float32)


def sum_kernel(where, mine, other, ket, *refs):
    minus, (out, bras, kets, total, arrived) = (refs[0] if len(refs) == 6 else None), refs[-5:]
    width = ket.shape[2]
    first, core = where[0], where[1]
    copies = []
    for n in range(8):
        source, h = ((mine, core), (other, 1 - core))[n % 2]
        j = n // 2
        copies.append(
            (
                pltpu.make_async_copy(
                    source.at[first + j, :, pl.ds(0, 2 * width)], bras.at[n], arrived.at[0, n]
                ),
                pltpu.make_async_copy(ket.at[pl.ds(4 * j + 2 * h, 2)], kets.at[n], arrived.at[1, n]),
            )
        )
    for pair in copies:
        for copy in pair:
            copy.start()
    for n, pair in enumerate(copies):
        for copy in pair:
            copy.wait()
        part = product_t(bras[n, :, :width], kets[n, 0])
        part = part + product_t(bras[n, :, width:], kets[n, 1])
        if n > 0:
            total[...] += part
        elif minus is None:
            total[...] = part
        else:
            total[...] = part - minus[...]
    out[...] = total[...].astype(out.dtype)


def partial_sum(mine, other, ket, group, core, dtype, minus=None):
    rows, (blocks, columns, width) = mine.shape[1], ket.shape
    where = jnp.stack([group * 4, core]).astype(jnp.int32)
    inside = pl.BlockSpec(memory_space=pltpu.VMEM)
    outside = pl.BlockSpec(memory_space=pltpu.HBM)
    more = () if minus is None else (minus,)
    return pl.pallas_call(
        sum_kernel,
        out_shape=jax.ShapeDtypeStruct((rows, columns), dtype),
        in_specs=[pl.BlockSpec(memory_space=pltpu.SMEM)] + [outside] * 3 + [inside] * len(more),
        out_specs=inside,
        scratch_shapes=[
            pltpu.VMEM((8, rows, 2 * width), mine.dtype),
            pltpu.VMEM((8, 2, columns, width), ket.dtype),
            pltpu.VMEM((rows, columns), jnp.float32),
            pltpu.SemaphoreType.DMA((2, 8)),
        ],
        compiler_params=pltpu.CompilerParams(vmem_limit_bytes=56 * 1024 * 1024),
        cost_estimate=pl.CostEstimate(
            flops=2 * rows * columns * blocks * width,
            bytes_accessed=2 * (rows + columns) * blocks * width,
            transcendentals=0,
        ),
    )(where, mine, other, ket, *more)


def local(bra_density, ket_density, coulomb, cond_pairs, val_pairs, screened, q_owner, g_shift):
    ylo = lax.axis_index("ylo")
    z = lax.axis_index("z")
    core = lax.axis_index("core")
    bra_index = lax.axis_index(ROW)
    ket_index = lax.axis_index(COL)
    cb_size = cond_pairs.shape[0]
    nc_size = cond_pairs.shape[2]
    nv_size = val_pairs.shape[1]
    vb_size = val_pairs.shape[2]
    ngw_size = val_pairs.shape[3]
    kbra = bra_index // (nc_size // cb_size)
    kket = ket_index // (nv_size // vb_size)
    rows, chunk = bra_density.shape
    half = ngw_size // 2

    ket = lax.all_gather(ket_density, "z", axis=0)

    gains = lax.dynamic_slice_in_dim(coulomb, ket_index * chunk, chunk)
    scaled = (bra_density.astype(jnp.float32) * gains[None, :]).astype(jnp.bfloat16) * 2
    moved = permute(scaled, lambda yl, zz, x, yh, c: (x // 2, zz, yl * 2 + x % 2, yh, c))

    q_index = q_owner[kbra, kket]
    w_half = lax.dynamic_slice_in_dim(screened[0], (z % 2) * half, half, 1)
    w_all = lax.all_to_all(
        jnp.broadcast_to(w_half[None], (8,) + w_half.shape), ("x", "yhi"), 0, 0, tiled=True
    )
    w_mine = lax.dynamic_index_in_dim(w_all, q_index // 2, 0, keepdims=False)
    w_other = permute(w_mine, lambda yl, zz, x, yh, c: (yl, zz, x, yh, 1 - c))
    w_mine = jnp.where(q_index % 2 == core, w_mine, w_other)
    w_other = permute(w_mine, lambda yl, zz, x, yh, c: (yl, zz ^ 1, x, yh, c))

    moved, w_mine = lax.optimization_barrier((moved, w_mine))
    spread = jnp.broadcast_to(moved[None], (8,) + moved.shape)
    mine = lax.all_to_all(spread, ("x", "yhi"), 0, 0, tiled=True)
    other = permute(mine, lambda yl, zz, x, yh, c: (yl, zz, x, yh, 1 - c))
    w_mine, w_other, val_pairs, cond_pairs, mine = lax.optimization_barrier(
        (w_mine, w_other, val_pairs, cond_pairs, mine)
    )
    w_block = jnp.concatenate(
        [jnp.where(z % 2 == 0, w_mine, w_other), jnp.where(z % 2 == 0, w_other, w_mine)], axis=1
    )
    perm = g_shift[kbra, kket]
    vals = lax.dynamic_index_in_dim(val_pairs, kbra, 0, keepdims=False)
    shifted = jnp.take(vals, perm, axis=2).reshape(nv_size * vb_size, ngw_size)
    pairs = lax.dot_general(
        shifted, w_block, (((1,), (1,)), ((), ())), preferred_element_type=jnp.float32
    )
    pairs = pairs.astype(jnp.bfloat16).reshape(nv_size, vb_size, ngw_size)
    conds = lax.dynamic_index_in_dim(cond_pairs, kket, 1, keepdims=False)
    direct = jnp.einsum("xcg,vug->vxuc", conds, pairs, preferred_element_type=jnp.float32)

    direct = direct.reshape(nv_size * cb_size, vb_size * nc_size)
    direct, ket = lax.optimization_barrier((direct, ket))
    send = partial_sum(mine, other, ket, 1 - ylo, core, jnp.bfloat16)
    got = permute(send, lambda yl, zz, x, yh, c: (1 - yl, zz, x, yh, c))
    keep = partial_sum(mine, other, ket, ylo, core, jnp.float32, direct)
    return keep + got.astype(jnp.float32)


def solution(mesh):
    fine = Mesh(mesh.devices.reshape(SIZES), AXES)
    return jax.shard_map(
        local,
        mesh=fine,
        in_specs=(
            P(ROW, COL),
            P(COL, ROW),
            P(),
            P(ROW, None, None, None),
            P(None, None, COL, None),
            P(COL, None, None),
            P(),
            P(),
        ),
        out_specs=P(ROW, COL),
        check_vma=False,
    )
```

```python
import functools

import jax
import jax.numpy as jnp
from jax import lax
from jax.experimental import pallas as pl
from jax.experimental.pallas import tpu as pltpu
from jax.sharding import Mesh, PartitionSpec as P

AXES = ("ylo", "z", "x", "yhi", "core")
SIZES = (2, 16, 4, 2, 2)
ROW = ("ylo", "z")
COL = ("x", "yhi", "core")


def flat(place):
    index = 0
    for at, size in zip(place, SIZES):
        index = index * size + at
    return index


def permute(array, target):
    pairs = []
    for ylo in range(2):
        for z in range(16):
            for x in range(4):
                for yhi in range(2):
                    for core in range(2):
                        place = (ylo, z, x, yhi, core)
                        pairs.append((flat(place), flat(target(*place))))
    return lax.ppermute(array, AXES, pairs)


def product_t(a, b):
    return lax.dot_general(a, b, (((1,), (1,)), ((), ())), preferred_element_type=jnp.float32)


def sum_kernel(turn, where, mine, other, ket, *refs):
    width = ket.shape[2]
    first, core = where[turn], where[2]
    if turn == 0:
        out, bras, kets, total, arrived = refs
    else:
        minus, out, bras, kets, total, arrived, less, less_arrived = refs
    copies = []
    for n in range(8):
        source, h = ((mine, core), (other, 1 - core))[n % 2]
        j = n // 2
        copies.append(
            (
                pltpu.make_async_copy(
                    source.at[first + j, :, pl.ds(0, 2 * width)], bras.at[n], arrived.at[0, n]
                ),
                pltpu.make_async_copy(ket.at[pl.ds(4 * j + 2 * h, 2)], kets.at[n], arrived.at[1, n]),
            )
        )
    for pair in copies:
        for copy in pair:
            copy.start()
    if turn == 1:
        last = pltpu.make_async_copy(minus, less, less_arrived)
        last.start()
    for n, pair in enumerate(copies):
        for copy in pair:
            copy.wait()
        part = product_t(bras[n, :, :width], kets[n, 0])
        part = part + product_t(bras[n, :, width:], kets[n, 1])
        if n == 0:
            total[...] = part
        elif n < 7:
            total[...] += part
        elif turn == 0:
            out[...] = (total[...] + part).astype(out.dtype)
        else:
            last.wait()
            out[...] = (total[...] + part) - less[...]


def partial_sum(turn, where, mine, other, ket, *minus):
    rows, (blocks, columns, width) = mine.shape[1], ket.shape
    inside = pl.BlockSpec(memory_space=pltpu.VMEM)
    outside = pl.BlockSpec(memory_space=pltpu.HBM)
    scratch = [
        pltpu.VMEM((8, rows, 2 * width), mine.dtype),
        pltpu.VMEM((8, 2, columns, width), ket.dtype),
        pltpu.VMEM((rows, columns), jnp.float32),
        pltpu.SemaphoreType.DMA((2, 8)),
    ]
    if turn == 1:
        scratch += [pltpu.VMEM((rows, columns), jnp.float32), pltpu.SemaphoreType.DMA]
    return pl.pallas_call(
        functools.partial(sum_kernel, turn),
        out_shape=jax.ShapeDtypeStruct((rows, columns), (jnp.bfloat16, jnp.float32)[turn]),
        in_specs=[pl.BlockSpec(memory_space=pltpu.SMEM)] + [outside] * (3 + len(minus)),
        out_specs=inside,
        scratch_shapes=scratch,
        compiler_params=pltpu.CompilerParams(vmem_limit_bytes=(56, 50)[turn] * 1024 * 1024),
        cost_estimate=pl.CostEstimate(
            flops=2 * rows * columns * blocks * width,
            bytes_accessed=2 * (rows + columns) * blocks * width,
            transcendentals=0,
        ),
    )(where, mine, other, ket, *minus)


def local(bra_density, ket_density, coulomb, cond_pairs, val_pairs, screened, q_owner, g_shift):
    ylo = lax.axis_index("ylo")
    z = lax.axis_index("z")
    core = lax.axis_index("core")
    bra_index = lax.axis_index(ROW)
    ket_index = lax.axis_index(COL)
    cb_size = cond_pairs.shape[0]
    nc_size = cond_pairs.shape[2]
    nv_size = val_pairs.shape[1]
    vb_size = val_pairs.shape[2]
    ngw_size = val_pairs.shape[3]
    kbra = bra_index // (nc_size // cb_size)
    kket = ket_index // (nv_size // vb_size)
    rows, chunk = bra_density.shape
    half = ngw_size // 2

    ket = lax.all_gather(ket_density, "z", axis=0)

    gains = lax.dynamic_slice_in_dim(coulomb, ket_index * chunk, chunk)
    scaled = (bra_density.astype(jnp.float32) * gains[None, :]).astype(jnp.bfloat16) * 2
    moved = permute(scaled, lambda yl, zz, x, yh, c: (x // 2, zz, yl * 2 + x % 2, yh, c))

    q_index = q_owner[kbra, kket]
    w_half = lax.dynamic_slice_in_dim(screened[0], (z % 2) * half, half, 1)
    w_all = lax.all_to_all(
        jnp.broadcast_to(w_half[None], (8,) + w_half.shape), ("x", "yhi"), 0, 0, tiled=True
    )
    w_mine = lax.dynamic_index_in_dim(w_all, q_index // 2, 0, keepdims=False)
    w_other = permute(w_mine, lambda yl, zz, x, yh, c: (yl, zz, x, yh, 1 - c))
    w_mine = jnp.where(q_index % 2 == core, w_mine, w_other)
    w_other = permute(w_mine, lambda yl, zz, x, yh, c: (yl, zz ^ 1, x, yh, c))

    moved, w_mine = lax.optimization_barrier((moved, w_mine))
    spread = jnp.broadcast_to(moved[None], (8,) + moved.shape)
    mine = lax.all_to_all(spread, ("x", "yhi"), 0, 0, tiled=True)
    other = permute(mine, lambda yl, zz, x, yh, c: (yl, zz, x, yh, 1 - c))
    w_mine, w_other, val_pairs, cond_pairs, mine = lax.optimization_barrier(
        (w_mine, w_other, val_pairs, cond_pairs, mine)
    )
    w_block = jnp.concatenate(
        [jnp.where(z % 2 == 0, w_mine, w_other), jnp.where(z % 2 == 0, w_other, w_mine)], axis=1
    )
    perm = g_shift[kbra, kket]
    vals = lax.dynamic_index_in_dim(val_pairs, kbra, 0, keepdims=False)
    shifted = jnp.take(vals, perm, axis=2).reshape(nv_size * vb_size, ngw_size)
    pairs = lax.dot_general(
        shifted, w_block, (((1,), (1,)), ((), ())), preferred_element_type=jnp.float32
    )
    pairs = pairs.astype(jnp.bfloat16).reshape(nv_size, vb_size, ngw_size)
    conds = lax.dynamic_index_in_dim(cond_pairs, kket, 1, keepdims=False)
    direct = jnp.einsum("xcg,vug->vxuc", conds, pairs, preferred_element_type=jnp.float32)

    direct = direct.reshape(nv_size * cb_size, vb_size * nc_size)
    where = jnp.stack([4 - 4 * ylo, 4 * ylo, core]).astype(jnp.int32)
    direct, ket, where = lax.optimization_barrier((direct, ket, where))
    send = partial_sum(0, where, mine, other, ket)
    got = permute(send, lambda yl, zz, x, yh, c: (1 - yl, zz, x, yh, c))
    keep = partial_sum(1, where, mine, other, ket, direct)
    return keep + got.astype(jnp.float32)


def solution(mesh):
    fine = Mesh(mesh.devices.reshape(SIZES), AXES)
    return jax.shard_map(
        local,
        mesh=fine,
        in_specs=(
            P(ROW, COL),
            P(COL, ROW),
            P(),
            P(ROW, None, None, None),
            P(None, None, COL, None),
            P(COL, None, None),
            P(),
            P(),
        ),
        out_specs=P(ROW, COL),
        check_vma=False,
    )
```

```python
import functools

import jax
import jax.numpy as jnp
from jax import lax
from jax.experimental import pallas as pl
from jax.experimental.pallas import tpu as pltpu
from jax.sharding import Mesh, PartitionSpec as P

AXES = ("ylo", "z", "x", "yhi", "core")
SIZES = (2, 16, 4, 2, 2)
ROW = ("ylo", "z")
COL = ("x", "yhi", "core")


def flat(place):
    index = 0
    for at, size in zip(place, SIZES):
        index = index * size + at
    return index


def permute(array, target):
    pairs = []
    for ylo in range(2):
        for z in range(16):
            for x in range(4):
                for yhi in range(2):
                    for core in range(2):
                        place = (ylo, z, x, yhi, core)
                        pairs.append((flat(place), flat(target(*place))))
    return lax.ppermute(array, AXES, pairs)


def product_t(a, b):
    return lax.dot_general(a, b, (((1,), (1,)), ((), ())), preferred_element_type=jnp.float32)


def sum_kernel(turn, where, mine, other, ket, *refs):
    width = ket.shape[2]
    first, core = where[turn], where[2]
    if turn == 0:
        out, bras, kets, total, arrived = refs
    else:
        minus, out, bras, kets, total, arrived, less, less_arrived = refs
    copies = []
    for n in range(8):
        source, h = ((mine, core), (other, 1 - core))[n % 2]
        j = n // 2
        copies.append(
            (
                pltpu.make_async_copy(
                    source.at[first + j, :, pl.ds(0, 2 * width)], bras.at[n], arrived.at[0, n]
                ),
                pltpu.make_async_copy(ket.at[pl.ds(4 * j + 2 * h, 2)], kets.at[n], arrived.at[1, n]),
            )
        )
    for pair in copies:
        for copy in pair:
            copy.start()
    if turn == 1:
        last = pltpu.make_async_copy(minus, less, less_arrived)
        last.start()
    for n, pair in enumerate(copies):
        for copy in pair:
            copy.wait()
        part = product_t(bras[n, :, :width], kets[n, 0])
        part = part + product_t(bras[n, :, width:], kets[n, 1])
        if n == 0:
            total[...] = part
        elif n < 7:
            total[...] += part
        elif turn == 0:
            out[...] = (total[...] + part).astype(out.dtype)
        else:
            last.wait()
            out[...] = (total[...] + part) - less[...]


def partial_sum(turn, where, mine, other, ket, *minus):
    rows, (blocks, columns, width) = mine.shape[1], ket.shape
    inside = pl.BlockSpec(memory_space=pltpu.VMEM)
    outside = pl.BlockSpec(memory_space=pltpu.HBM)
    scratch = [
        pltpu.VMEM((8, rows, 2 * width), mine.dtype),
        pltpu.VMEM((8, 2, columns, width), ket.dtype),
        pltpu.VMEM((rows, columns), jnp.float32),
        pltpu.SemaphoreType.DMA((2, 8)),
    ]
    if turn == 1:
        scratch += [pltpu.VMEM((rows, columns), jnp.float32), pltpu.SemaphoreType.DMA]
    return pl.pallas_call(
        functools.partial(sum_kernel, turn),
        out_shape=jax.ShapeDtypeStruct((rows, columns), (jnp.bfloat16, jnp.float32)[turn]),
        in_specs=[pl.BlockSpec(memory_space=pltpu.SMEM)] + [outside] * (3 + len(minus)),
        out_specs=inside,
        scratch_shapes=scratch,
        compiler_params=pltpu.CompilerParams(vmem_limit_bytes=50 * 1024 * 1024),
        cost_estimate=pl.CostEstimate(
            flops=2 * rows * columns * blocks * width,
            bytes_accessed=2 * (rows + columns) * blocks * width,
            transcendentals=0,
        ),
    )(where, mine, other, ket, *minus)


def local(bra_density, ket_density, coulomb, cond_pairs, val_pairs, screened, q_owner, g_shift):
    ylo = lax.axis_index("ylo")
    z = lax.axis_index("z")
    core = lax.axis_index("core")
    bra_index = lax.axis_index(ROW)
    ket_index = lax.axis_index(COL)
    cb_size = cond_pairs.shape[0]
    nc_size = cond_pairs.shape[2]
    nv_size = val_pairs.shape[1]
    vb_size = val_pairs.shape[2]
    ngw_size = val_pairs.shape[3]
    kbra = bra_index // (nc_size // cb_size)
    kket = ket_index // (nv_size // vb_size)
    rows, chunk = bra_density.shape
    half = ngw_size // 2

    ket = lax.all_gather(ket_density, "z", axis=0)

    gains = lax.dynamic_slice_in_dim(coulomb, ket_index * chunk, chunk)
    scaled = (bra_density.astype(jnp.float32) * gains[None, :]).astype(jnp.bfloat16) * 2
    moved = permute(scaled, lambda yl, zz, x, yh, c: (x // 2, zz, yl * 2 + x % 2, yh, c))

    q_index = q_owner[kbra, kket]
    w_half = lax.dynamic_slice_in_dim(screened[0], (z % 2) * half, half, 1)
    w_all = lax.all_to_all(
        jnp.broadcast_to(w_half[None], (8,) + w_half.shape), ("x", "yhi"), 0, 0, tiled=True
    )
    w_mine = lax.dynamic_index_in_dim(w_all, q_index // 2, 0, keepdims=False)
    w_other = permute(w_mine, lambda yl, zz, x, yh, c: (yl, zz, x, yh, 1 - c))
    w_mine = jnp.where(q_index % 2 == core, w_mine, w_other)
    w_other = permute(w_mine, lambda yl, zz, x, yh, c: (yl, zz ^ 1, x, yh, c))

    moved, w_mine = lax.optimization_barrier((moved, w_mine))
    spread = jnp.broadcast_to(moved[None], (8,) + moved.shape)
    mine = lax.all_to_all(spread, ("x", "yhi"), 0, 0, tiled=True)
    other = permute(mine, lambda yl, zz, x, yh, c: (yl, zz, x, yh, 1 - c))
    w_mine, w_other, val_pairs, cond_pairs, mine = lax.optimization_barrier(
        (w_mine, w_other, val_pairs, cond_pairs, mine)
    )
    w_block = jnp.concatenate(
        [jnp.where(z % 2 == 0, w_mine, w_other), jnp.where(z % 2 == 0, w_other, w_mine)], axis=1
    )
    perm = g_shift[kbra, kket]
    vals = lax.dynamic_index_in_dim(val_pairs, kbra, 0, keepdims=False)
    shifted = jnp.take(vals, perm, axis=2).reshape(nv_size * vb_size, ngw_size)
    pairs = lax.dot_general(
        shifted, w_block, (((1,), (1,)), ((), ())), preferred_element_type=jnp.float32
    )
    pairs = pairs.astype(jnp.bfloat16).reshape(nv_size, vb_size, ngw_size)
    conds = lax.dynamic_index_in_dim(cond_pairs, kket, 1, keepdims=False)
    direct = jnp.einsum("xcg,vug->vxuc", conds, pairs, preferred_element_type=jnp.float32)

    direct = direct.reshape(nv_size * cb_size, vb_size * nc_size)
    where = jnp.stack([4 - 4 * ylo, 4 * ylo, core]).astype(jnp.int32)
    direct, ket, where = lax.optimization_barrier((direct, ket, where))
    send = partial_sum(0, where, mine, other, ket)
    got = permute(send, lambda yl, zz, x, yh, c: (1 - yl, zz, x, yh, c))
    keep = partial_sum(1, where, mine, other, ket, direct)
    return keep + got.astype(jnp.float32)


def solution(mesh):
    fine = Mesh(mesh.devices.reshape(SIZES), AXES)
    return jax.shard_map(
        local,
        mesh=fine,
        in_specs=(
            P(ROW, COL),
            P(COL, ROW),
            P(),
            P(ROW, None, None, None),
            P(None, None, COL, None),
            P(COL, None, None),
            P(),
            P(),
        ),
        out_specs=P(ROW, COL),
        check_vma=False,
    )
```

```python
import functools

import jax
import jax.numpy as jnp
from jax import lax
from jax.experimental import pallas as pl
from jax.experimental.pallas import tpu as pltpu
from jax.sharding import Mesh, PartitionSpec as P

AXES = ("ylo", "z", "x", "yhi", "core")
SIZES = (2, 16, 4, 2, 2)
ROW = ("ylo", "z")
COL = ("x", "yhi", "core")


def flat(place):
    index = 0
    for at, size in zip(place, SIZES):
        index = index * size + at
    return index


def permute(array, target):
    pairs = []
    for ylo in range(2):
        for z in range(16):
            for x in range(4):
                for yhi in range(2):
                    for core in range(2):
                        place = (ylo, z, x, yhi, core)
                        pairs.append((flat(place), flat(target(*place))))
    return lax.ppermute(array, AXES, pairs)


def product_t(a, b):
    return lax.dot_general(a, b, (((1,), (1,)), ((), ())), preferred_element_type=jnp.float32)


def sum_kernel(turn, where, mine, other, ket, *refs):
    width = ket.shape[2]
    first, core = where[turn], where[2]
    if turn == 0:
        out, bras, kets, total, arrived = refs
    else:
        minus, out, bras, kets, total, arrived, less, less_arrived = refs
    copies = []
    for n in range(8):
        source, h = ((mine, core), (other, 1 - core))[n % 2]
        j = n // 2
        copies.append(
            (
                pltpu.make_async_copy(
                    source.at[first + j, :, pl.ds(0, 2 * width)], bras.at[n], arrived.at[0, n]
                ),
                pltpu.make_async_copy(ket.at[pl.ds(4 * j + 2 * h, 2)], kets.at[n], arrived.at[1, n]),
            )
        )
    for pair in copies:
        for copy in pair:
            copy.start()
    if turn == 1:
        last = pltpu.make_async_copy(minus, less, less_arrived)
        last.start()
    for n, pair in enumerate(copies):
        for copy in pair:
            copy.wait()
        part = product_t(bras[n, :, :width], kets[n, 0])
        part = part + product_t(bras[n, :, width:], kets[n, 1])
        if n == 0:
            total[...] = part
        elif n < 7:
            total[...] += part
        elif turn == 0:
            out[...] = (total[...] + part).astype(out.dtype)
        else:
            last.wait()
            out[...] = (total[...] + part) - less[...]


def partial_sum(turn, where, mine, other, ket, *minus):
    rows, (blocks, columns, width) = mine.shape[1], ket.shape
    inside = pl.BlockSpec(memory_space=pltpu.VMEM)
    outside = pl.BlockSpec(memory_space=pltpu.HBM)
    scratch = [
        pltpu.VMEM((8, rows, 2 * width), mine.dtype),
        pltpu.VMEM((8, 2, columns, width), ket.dtype),
        pltpu.VMEM((rows, columns), jnp.float32),
        pltpu.SemaphoreType.DMA((2, 8)),
    ]
    if turn == 1:
        scratch += [pltpu.VMEM((rows, columns), jnp.float32), pltpu.SemaphoreType.DMA]
    return pl.pallas_call(
        functools.partial(sum_kernel, turn),
        out_shape=jax.ShapeDtypeStruct((rows, columns), (jnp.bfloat16, jnp.float32)[turn]),
        in_specs=[pl.BlockSpec(memory_space=pltpu.SMEM)] + [outside] * (3 + len(minus)),
        out_specs=inside,
        scratch_shapes=scratch,
        compiler_params=pltpu.CompilerParams(vmem_limit_bytes=50 * 1024 * 1024),
        cost_estimate=pl.CostEstimate(
            flops=2 * rows * columns * blocks * width,
            bytes_accessed=2 * (rows + columns) * blocks * width,
            transcendentals=0,
        ),
    )(where, mine, other, ket, *minus)


def local(bra_density, ket_density, coulomb, cond_pairs, val_pairs, screened, q_owner, g_shift):
    ylo = lax.axis_index("ylo")
    z = lax.axis_index("z")
    core = lax.axis_index("core")
    bra_index = lax.axis_index(ROW)
    ket_index = lax.axis_index(COL)
    cb_size = cond_pairs.shape[0]
    nc_size = cond_pairs.shape[2]
    nv_size = val_pairs.shape[1]
    vb_size = val_pairs.shape[2]
    ngw_size = val_pairs.shape[3]
    kbra = bra_index // (nc_size // cb_size)
    kket = ket_index // (nv_size // vb_size)
    rows, chunk = bra_density.shape
    half = ngw_size // 2

    ket = lax.all_gather(ket_density, "z", axis=0)

    gains = lax.dynamic_slice_in_dim(coulomb, ket_index * chunk, chunk)
    scaled = (bra_density.astype(jnp.float32) * gains[None, :]).astype(jnp.bfloat16) * 2
    moved = permute(scaled, lambda yl, zz, x, yh, c: (x // 2, zz, yl * 2 + x % 2, yh, c))

    q_index = q_owner[kbra, kket]
    w_half = lax.dynamic_slice_in_dim(screened[0], (z % 2) * half, half, 1)
    w_all = lax.all_to_all(
        jnp.broadcast_to(w_half[None], (8,) + w_half.shape), ("x", "yhi"), 0, 0, tiled=True
    )
    w_mine = lax.dynamic_index_in_dim(w_all, q_index // 2, 0, keepdims=False)
    w_other = permute(w_mine, lambda yl, zz, x, yh, c: (yl, zz, x, yh, 1 - c))
    w_mine = jnp.where(q_index % 2 == core, w_mine, w_other)
    w_other = permute(w_mine, lambda yl, zz, x, yh, c: (yl, zz ^ 1, x, yh, c))

    moved, w_mine, w_other = lax.optimization_barrier((moved, w_mine, w_other))
    spread = jnp.broadcast_to(moved[None], (8,) + moved.shape)
    mine = lax.all_to_all(spread, ("x", "yhi"), 0, 0, tiled=True)
    other = permute(mine, lambda yl, zz, x, yh, c: (yl, zz, x, yh, 1 - c))
    w_mine, w_other, val_pairs, cond_pairs, mine = lax.optimization_barrier(
        (w_mine, w_other, val_pairs, cond_pairs, mine)
    )
    w_block = jnp.concatenate(
        [jnp.where(z % 2 == 0, w_mine, w_other), jnp.where(z % 2 == 0, w_other, w_mine)], axis=1
    )
    perm = g_shift[kbra, kket]
    vals = lax.dynamic_index_in_dim(val_pairs, kbra, 0, keepdims=False)
    shifted = jnp.take(vals, perm, axis=2).reshape(nv_size * vb_size, ngw_size)
    pairs = lax.dot_general(
        shifted, w_block, (((1,), (1,)), ((), ())), preferred_element_type=jnp.float32
    )
    pairs = pairs.astype(jnp.bfloat16).reshape(nv_size, vb_size, ngw_size)
    conds = lax.dynamic_index_in_dim(cond_pairs, kket, 1, keepdims=False)
    direct = jnp.einsum("xcg,vug->vxuc", conds, pairs, preferred_element_type=jnp.float32)

    direct = direct.reshape(nv_size * cb_size, vb_size * nc_size)
    where = jnp.stack([4 - 4 * ylo, 4 * ylo, core]).astype(jnp.int32)
    direct, ket, where = lax.optimization_barrier((direct, ket, where))
    send = partial_sum(0, where, mine, other, ket)
    got = permute(send, lambda yl, zz, x, yh, c: (1 - yl, zz, x, yh, c))
    keep = partial_sum(1, where, mine, other, ket, direct)
    return keep + got.astype(jnp.float32)


def solution(mesh):
    fine = Mesh(mesh.devices.reshape(SIZES), AXES)
    return jax.shard_map(
        local,
        mesh=fine,
        in_specs=(
            P(ROW, COL),
            P(COL, ROW),
            P(),
            P(ROW, None, None, None),
            P(None, None, COL, None),
            P(COL, None, None),
            P(),
            P(),
        ),
        out_specs=P(ROW, COL),
        check_vma=False,
    )
```
